512 devices in a mesh: rep: 32 (over x, y_hi, core), tp: 8 (over z), seq: 2 (over y_lo).
Axes of the slice: x: 4, y: 8 (y_hi: 4, y_lo: 2; y = y_hi * 2 + y_lo), z: 8, core: 2. Of those that a mesh axis runs over, the one named last changes fastest.
Arguments:
- tokens: bfloat16 [32, 640, 4096], P('rep', 'seq', 'tp'), may hold values from -6 to 6
- queries: bfloat16 [32, 640, 4096], P('rep', 'seq', 'tp'), may hold values from -256 to 256
- output_gradient: bfloat16 [32, 640, 4096], P('rep', 'seq', 'tp'), may hold values from -6 to 6
- key_matrix: bfloat16 [32, 4096, 1024], P('rep', 'seq', 'tp'), may hold values from -0.09375 to 0.09375
- value_matrix: bfloat16 [32, 4096, 1024], P('rep', 'seq', 'tp'), may hold values from -0.09375 to 0.09375
- key_velocity: bfloat16 [32, 4096, 1024], P('rep', 'seq', 'tp'), may hold values from -6 to 6
- value_velocity: bfloat16 [32, 4096, 1024], P('rep', 'seq', 'tp'), may hold values from -6 to 6
- partner_bit: int32 [1], replicated, may hold values from 0 to 1048575
Outputs:
- key_weight_out: bfloat16 [32, 4096, 1024], P('rep', 'seq', 'tp')
- value_weight_out: bfloat16 [32, 4096, 1024], P('rep', 'seq', 'tp')
- key_moment_out: bfloat16 [32, 4096, 1024], P('rep', 'seq', 'tp')
- value_moment_out: bfloat16 [32, 4096, 1024], P('rep', 'seq', 'tp')
The draws below stay inside these ranges and needn't reach their ends.
All inputs are finite; a program needn't handle non-finite values.
Results may differ from the reference program's by a relative error of at most 0.017.
The reference program's roundings to bfloat16 on the way (of `probs_low` and `score_grad`) count: a program that leaves them out, or rounds other values in their place, can miss the bound.
Values may be sent and summed in bfloat16 or wider, within the bound.
No kernel may reach another device: no remote copies, remote signals or barrier semaphores. Data moves between devices by JAX's collectives and lax.ppermute only.
A program may use at most 64 MiB of HBM per device.

```python
import math
import jax
import jax.numpy as jnp
from jax import lax

MODEL_WIDTH = 4096
QUERY_HEADS = 32
KEY_VALUE_HEADS = 8
HEAD_SIZE = 128
SEQ_LEN = 640
REPLICA_COUNT = 32
REP_BITS = 5
N_SEQ = 2


def draw_queries(key, part):
    key = jax.random.fold_in(key, 7)
    normal_draw = jnp.clip(jax.random.normal(key, (REPLICA_COUNT, SEQ_LEN, QUERY_HEADS * HEAD_SIZE), jnp.float32), -4.0, 4.0)
    return normal_draw.astype(jnp.bfloat16)


def draw_output_gradient(key, part):
    key = jax.random.fold_in(key, 13)
    normal_draw = jnp.clip(jax.random.normal(key, (REPLICA_COUNT, SEQ_LEN, QUERY_HEADS * HEAD_SIZE), jnp.float32), -6.0, 6.0)
    return normal_draw.astype(jnp.bfloat16)


def block_levels(stream_key, extent, cuts, low, top_value):
    loudness, own = 1.0, jax.random.fold_in(stream_key, 6)
    for axis_at, shards_of in cuts:
        heights = jnp.exp(jax.random.uniform(jax.random.fold_in(own, axis_at), (shards_of,), jnp.float32, low / len(cuts), top_value / len(cuts)))
        loudness = loudness * jnp.repeat(heights, extent[axis_at] // shards_of).reshape([-1 if axis == axis_at else 1 for axis in range(len(extent))])
    return loudness


def normal_values(own_key, shape, spread, most, split=(), held_as=jnp.bfloat16):
    result = jax.random.normal(own_key, shape, jnp.float32) * spread
    if len(split) > 0:
        result = block_levels(own_key, shape, split, -0.22, 0.18) * result
    return jnp.clip(result, min=-most, max=most).astype(held_as)


def setup_inputs(seed: int = 0) -> dict:
    keys = jax.random.split(jax.random.key(seed), 9)
    return {
        "tokens": normal_values(keys[0], (REPLICA_COUNT, SEQ_LEN, MODEL_WIDTH), 1.0, 6.0, ((0, 32), (1, 2), (2, 8))),
        "queries": draw_queries(jax.random.fold_in(keys[8], 71), 0),
        "output_gradient": draw_output_gradient(jax.random.fold_in(keys[8], 71), 0),
        "key_matrix": normal_values(keys[3], (REPLICA_COUNT, MODEL_WIDTH, KEY_VALUE_HEADS * HEAD_SIZE), MODEL_WIDTH ** -0.5, 0.09375, ((0, 32), (1, 2), (2, 8))),
        "value_matrix": normal_values(keys[4], (REPLICA_COUNT, MODEL_WIDTH, KEY_VALUE_HEADS * HEAD_SIZE), MODEL_WIDTH ** -0.5, 0.09375, ((0, 32), (1, 2), (2, 8))),
        "key_velocity": normal_values(keys[5], (REPLICA_COUNT, MODEL_WIDTH, KEY_VALUE_HEADS * HEAD_SIZE), 1.0, 6.0, ((0, 32), (1, 2), (2, 8))),
        "value_velocity": normal_values(keys[6], (REPLICA_COUNT, MODEL_WIDTH, KEY_VALUE_HEADS * HEAD_SIZE), 1.0, 6.0, ((0, 32), (1, 2), (2, 8))),
        "partner_bit": jax.random.randint(keys[7], (1,), 0, 1048576).astype(jnp.int32),
    }


MOMENTUM = 0.9
LEARN_RATE = 0.01

def replica_grads(inputs):
    tokens, queries, output_gradient, key_matrix, value_matrix = inputs
    length_total = tokens.shape[0]
    group_width = QUERY_HEADS // KEY_VALUE_HEADS
    score_scale = 1.0 / math.sqrt(HEAD_SIZE)
    key_row_block = jnp.dot(tokens, key_matrix, preferred_element_type=jnp.float32).astype(jnp.bfloat16)
    value_row_block = jnp.dot(tokens, value_matrix, preferred_element_type=jnp.float32).astype(jnp.bfloat16)
    query_head_rows = queries.astype(jnp.float32).reshape(length_total, KEY_VALUE_HEADS, group_width, HEAD_SIZE)
    key_head_rows = key_row_block.astype(jnp.float32).reshape(length_total, KEY_VALUE_HEADS, HEAD_SIZE)
    value_head_rows = value_row_block.astype(jnp.float32).reshape(length_total, KEY_VALUE_HEADS, HEAD_SIZE)
    scores = jnp.einsum('ihgd,jhd->hgij', query_head_rows, key_head_rows) * score_scale
    causal = jnp.arange(length_total)[:, None] >= jnp.arange(length_total)[None, :]
    scores = jnp.where(causal, scores, jnp.float32(-1e+30))
    row_peak = lax.optimization_barrier(jnp.max(scores, axis=-1, keepdims=True))
    exponent = jnp.where(causal, jnp.exp(scores - row_peak), jnp.float32(0.0))
    probs = exponent / lax.optimization_barrier(jnp.sum(exponent, axis=-1, keepdims=True))
    probs_low = lax.optimization_barrier(probs.astype(jnp.bfloat16)).astype(jnp.float32)
    context = jnp.einsum('hgij,jhd->ihgd', probs_low, value_head_rows)
    gradient_heads = output_gradient.astype(jnp.float32).reshape(length_total, KEY_VALUE_HEADS, group_width, HEAD_SIZE)
    value_gradient = jnp.einsum('hgij,ihgd->jhd', probs_low, gradient_heads)
    prob_grad = jnp.einsum('ihgd,jhd->hgij', gradient_heads, value_head_rows)
    out_dot = jnp.transpose(lax.optimization_barrier(jnp.sum(gradient_heads * context, axis=-1)), (1, 2, 0))
    score_grad = probs * (prob_grad - out_dot[..., None])
    score_grad = lax.optimization_barrier(score_grad.astype(jnp.bfloat16)).astype(jnp.float32)
    key_gradient = jnp.einsum('hgij,ihgd->jhd', score_grad, query_head_rows) * score_scale
    key_reduced = key_gradient.reshape(length_total, KEY_VALUE_HEADS * HEAD_SIZE).astype(jnp.bfloat16)
    value_reduced = value_gradient.reshape(length_total, KEY_VALUE_HEADS * HEAD_SIZE).astype(jnp.bfloat16)
    block_rows = length_total // N_SEQ
    gradient_key = jnp.zeros((tokens.shape[1], KEY_VALUE_HEADS * HEAD_SIZE), jnp.float32)
    gradient_value = jnp.zeros((tokens.shape[1], KEY_VALUE_HEADS * HEAD_SIZE), jnp.float32)
    for block in range(N_SEQ):
        token_block = tokens[block * block_rows:(block + 1) * block_rows]
        part_key = jnp.dot(token_block.T, key_reduced[block * block_rows:(block + 1) * block_rows], preferred_element_type=jnp.float32)
        part_value = jnp.dot(token_block.T, value_reduced[block * block_rows:(block + 1) * block_rows], preferred_element_type=jnp.float32)
        gradient_key = gradient_key + lax.optimization_barrier(part_key.astype(jnp.bfloat16)).astype(jnp.float32)
        gradient_value = gradient_value + lax.optimization_barrier(part_value.astype(jnp.bfloat16)).astype(jnp.float32)
    return (gradient_key, gradient_value)

def average_pair(weight, moment, grad, partner):
    moment_f = moment.astype(jnp.float32)
    weight_f = weight.astype(jnp.float32)
    moment_new = MOMENTUM * 0.5 * (moment_f + moment_f[partner]) + 0.5 * (grad + grad[partner])
    weight_new = 0.5 * (weight_f + weight_f[partner]) - LEARN_RATE * moment_new
    return (weight_new.astype(jnp.bfloat16), moment_new.astype(jnp.bfloat16))

def reference(tokens, queries, output_gradient, key_matrix, value_matrix, key_velocity, value_velocity, partner_bit):
    gradient_key, gradient_value = lax.map(replica_grads, (tokens, queries, output_gradient, key_matrix, value_matrix))
    exponent_bit = jnp.remainder(partner_bit[0].astype(jnp.int32), jnp.int32(REP_BITS))
    distance = jnp.left_shift(jnp.int32(1), exponent_bit)
    partner = jnp.bitwise_xor(jnp.arange(REPLICA_COUNT, dtype=jnp.int32), distance)
    key_weight_out, key_moment_out = average_pair(key_matrix, key_velocity, gradient_key, partner)
    value_weight_out, value_moment_out = average_pair(value_matrix, value_velocity, gradient_value, partner)
    return (key_weight_out, value_weight_out, key_moment_out, value_moment_out)
```

```python
import functools
import math

import jax
import jax.numpy as jnp
from jax import lax
from jax.experimental import pallas as pl
from jax.experimental.pallas import tpu as pltpu
from jax.sharding import PartitionSpec as P

HEAD_SIZE = 128
GROUP = 4
MOMENTUM = 0.9
LEARN_RATE = 0.01
SCORE_SCALE = 1.0 / math.sqrt(HEAD_SIZE)
F32 = jnp.float32
BF16 = jnp.bfloat16
VMEM = pl.BlockSpec(memory_space=pltpu.VMEM)
SMEM = pl.BlockSpec(memory_space=pltpu.SMEM)


def nt(a, b):
    return lax.dot_general(a, b, (((1,), (1,)), ((), ())), preferred_element_type=F32)


def tn(a, b):
    return lax.dot_general(a, b, (((0,), (0,)), ((), ())), preferred_element_type=F32)


def nn(a, b):
    return jnp.dot(a, b, preferred_element_type=F32)


def call(kernel, outs, args, scratch=(), flops=0, limit=32):
    moved = sum(math.prod(a.shape) * a.dtype.itemsize for a in (*outs, *args))
    return pl.pallas_call(
        kernel,
        out_shape=outs,
        in_specs=[SMEM] + [VMEM] * (len(args) - 1),
        out_specs=[VMEM] * len(outs),
        scratch_shapes=list(scratch),
        compiler_params=pltpu.CompilerParams(vmem_limit_bytes=limit << 20),
        cost_estimate=pl.CostEstimate(flops=flops, bytes_accessed=moved, transcendentals=0),
    )(*args)


def project_kernel(place, *refs):
    blocks, (w_own, w_other, kv_out, half_out, total) = refs[:8], refs[8:]
    seq = place[0]
    depth = blocks[0].shape[1]
    per_half = w_own.shape[0] // depth
    for k, block in enumerate(blocks):
        feature = place[1 + k]
        side = feature // per_half
        at = feature - side * per_half
        rows = pl.ds(pl.multiple_of(at * depth, depth), depth)

        @pl.when(side == seq)
        def _():
            part = nn(block[...], w_own[rows, :])
            total[...] = part if k == 0 else total[...] + part
            half_out[at] = block[...]

        @pl.when(side != seq)
        def _():
            part = nn(block[...], w_other[rows, :])
            total[...] = part if k == 0 else total[...] + part

    kv_out[...] = total[...].astype(BF16)


def attention_kernel(place, q_own, do_own, qdo_other, kv_own, kv_other, d_own, d_other, q_all, do_all, kv_all, d_all):
    seq = place[0]
    other = 1 - seq
    rows = q_own.shape[0]
    width = q_own.shape[1]
    for h in range(GROUP):
        at, col = pl.ds(h * rows, rows), pl.ds(h * HEAD_SIZE, HEAD_SIZE)
        q_all[seq, at, :] = q_own[:, col]
        do_all[seq, at, :] = do_own[:, col]
        q_all[other, at, :] = qdo_other[:, col]
        do_all[other, at, :] = qdo_other[:, pl.ds(width + h * HEAD_SIZE, HEAD_SIZE)]
    kv_all[seq] = kv_own[...]
    kv_all[other] = kv_other[...]
    span = 2 * rows
    key_at = lax.broadcasted_iota(jnp.int32, (rows, span), 0)
    query_at = lax.broadcasted_iota(jnp.int32, (rows, span), 1)
    query_at = jnp.where(query_at >= rows, query_at - rows, query_at)
    causal = key_at <= query_at
    d_all[...] = jnp.zeros_like(d_all)
    for block in range(2):
        for chunk in range(GROUP * rows // span):
            q = q_all[block, pl.ds(chunk * span, span), :]
            do = do_all[block, pl.ds(chunk * span, span), :]
            scores = []
            for j in range(block + 1):
                s = nt(kv_all[j, :, :HEAD_SIZE], q) * SCORE_SCALE
                scores.append(jnp.where(causal, s, F32(-1e30)) if j == block else s)
            peak = functools.reduce(jnp.maximum, [jnp.max(s, axis=0, keepdims=True) for s in scores])
            weights = [jnp.exp(s - peak) for s in scores]
            share = 1.0 / sum(jnp.sum(e, axis=0, keepdims=True) for e in weights)
            probs = [e * share for e in weights]
            low = [p.astype(BF16) for p in probs]
            grads = [nt(kv_all[j, :, HEAD_SIZE:], do) for j in range(block + 1)]
            dot = sum(jnp.sum(p.astype(F32) * g, axis=0, keepdims=True) for p, g in zip(low, grads))
            for j in range(block + 1):
                score_grad = (probs[j] * (grads[j] - dot)).astype(BF16)
                d_all[j, :, :HEAD_SIZE] += nn(score_grad, q)
                d_all[j, :, HEAD_SIZE:] += nn(low[j], do)

    def reduced(at, out):
        out[:, :HEAD_SIZE] = (d_all[at, :, :HEAD_SIZE] * SCORE_SCALE).astype(BF16)
        out[:, HEAD_SIZE:] = d_all[at, :, HEAD_SIZE:].astype(BF16)

    reduced(seq, d_own)
    reduced(other, d_other)


def moment_kernel(place, x_half, x_other, d_own, d_other, key_m, value_m, key_f, value_f, key_low, value_low):
    seq = place[0]
    groups, rows, depth = x_half.shape
    lines = rows // 2
    for i in range(groups):
        at = pl.ds(i * depth, depth)
        own = tn(x_half[i], d_own[...])
        a, b = seq * groups + i, (1 - seq) * groups + i
        far = tn(x_other[a], d_other[:lines, :]) + tn(x_other[b], d_other[lines:, :])
        grad = own.astype(BF16).astype(F32) + far.astype(BF16).astype(F32)
        for m, f, low, cols in (
            (key_m, key_f, key_low, slice(0, HEAD_SIZE)),
            (value_m, value_f, value_low, slice(HEAD_SIZE, 2 * HEAD_SIZE)),
        ):
            moment = MOMENTUM * m[at, :].astype(F32) + grad[:, cols]
            f[at, :] = moment
            low[at, :] = moment.astype(BF16)


def shifted(block, distance):
    count = lax.axis_size("tp")
    return lax.ppermute(block, "tp", [(i, (i + distance) % count) for i in range(count)])


def swapped(block, axis, distance):
    return lax.ppermute(block, axis, [(i, i ^ distance) for i in range(lax.axis_size(axis))])


def crossed(block):
    count = lax.axis_size("tp")
    half = count // 2
    lines = block.shape[0] // 2
    senders = [(t, s) for t in range(count) for s in range(2) if t // half != s]
    first = lax.ppermute(block[:lines], ("tp", "seq"), [(2 * t + s, 2 * t + 1 - s) for t, s in senders])
    second = lax.ppermute(
        block[lines:], ("tp", "seq"), [(2 * t + s, 2 * ((t + half) % count) + 1 - s) for t, s in senders]
    )
    mine = lax.axis_index("tp") // half == lax.axis_index("seq")
    return jnp.where(mine, first, second)


def step(bit, tokens, queries, output_gradient, key_matrix, value_matrix, key_velocity, value_velocity):
    tokens, queries, output_gradient = tokens[0], queries[0], output_gradient[0]
    key_w, value_w, key_m, value_m = key_matrix[0], value_matrix[0], key_velocity[0], value_velocity[0]
    rows, depth = tokens.shape
    features, head = key_w.shape
    count = lax.axis_size("tp")
    seq, tp = lax.axis_index("seq"), lax.axis_index("tp")

    right, left = [tokens], []
    for k in range(count // 2):
        right.append(shifted(right[-1], 1))
        if k < count // 2 - 1:
            left.append(shifted(left[-1] if left else tokens, -1))
    blocks = right + left
    offsets = [k for k in range(len(right))] + [-1 - k for k in range(len(left))]
    place = jnp.stack([seq] + [jnp.remainder(tp - k + count, count) for k in offsets]).astype(jnp.int32)

    weights = jnp.concatenate([key_w, value_w], axis=1)
    weights_other = swapped(weights, "seq", 1)
    x_other = lax.all_gather(crossed(tokens), "tp", axis=0, tiled=False)
    qdo_other = swapped(jnp.concatenate([queries, output_gradient], axis=1), "seq", 1)
    weights_partner = swapped(weights, "rep", 1 << bit)

    shape = jax.ShapeDtypeStruct
    kv, x_half = call(
        project_kernel,
        [shape((rows, 2 * head), BF16), shape((count // 2, rows, depth), BF16)],
        [place, *blocks, weights, weights_other],
        [pltpu.VMEM((rows, 2 * head), F32)],
        flops=2 * rows * 2 * features * 2 * head,
    )
    kv_other = swapped(kv, "seq", 1)
    wide = pltpu.VMEM((2, GROUP * rows, head), BF16)
    d_own, d_other = call(
        attention_kernel,
        [shape((rows, 2 * head), BF16)] * 2,
        [place, queries, output_gradient, qdo_other, kv, kv_other],
        [wide, wide, pltpu.VMEM((2, rows, 2 * head), BF16), pltpu.VMEM((2, rows, 2 * head), F32)],
        flops=2 * 4 * 3 * GROUP * rows * rows * head,
    )
    key_f, value_f, key_low, value_low = call(
        moment_kernel,
        [shape((features, head), F32)] * 2 + [shape((features, head), BF16)] * 2,
        [place, x_half, x_other, d_own, d_other, key_m, value_m],
        flops=2 * 2 * rows * features * 2 * head,
    )
    key_far = swapped(key_low, "rep", 1 << bit)
    value_far = swapped(value_low, "rep", 1 << bit)

    def averaged(weight, weight_far, moment, moment_far):
        moment_new = 0.5 * (moment + moment_far.astype(F32))
        weight_new = 0.5 * (weight.astype(F32) + weight_far.astype(F32)) - LEARN_RATE * moment_new
        return weight_new.astype(BF16)[None], moment_new.astype(BF16)[None]

    key_w_new, key_m_new = averaged(key_w, weights_partner[:, :head], key_f, key_far)
    value_w_new, value_m_new = averaged(value_w, weights_partner[:, head:], value_f, value_far)
    return key_w_new, value_w_new, key_m_new, value_m_new


def per_device(*args):
    levels = lax.axis_size("rep").bit_length() - 1
    which = jnp.remainder(args[-1][0], jnp.int32(levels))
    return lax.switch(which, [functools.partial(step, bit) for bit in range(levels)], *args[:-1])


def solution(mesh):
    split = P("rep", "seq", "tp")
    return jax.shard_map(
        per_device,
        mesh=mesh,
        in_specs=(split,) * 7 + (P(),),
        out_specs=(split,) * 4,
        check_vma=False,
    )
```

```python
import functools
import math

import jax
import jax.numpy as jnp
from jax import lax
from jax.experimental import pallas as pl
from jax.experimental.pallas import tpu as pltpu
from jax.sharding import PartitionSpec as P

HEAD_SIZE = 128
GROUP = 4
PARTS = 4
CROWDED = (1, 2)
MOMENTUM = 0.9
LEARN_RATE = 0.01
SCORE_SCALE = 1.0 / math.sqrt(HEAD_SIZE)
F32 = jnp.float32
BF16 = jnp.bfloat16
VMEM = pl.BlockSpec(memory_space=pltpu.VMEM)
SMEM = pl.BlockSpec(memory_space=pltpu.SMEM)


def nt(a, b):
    return lax.dot_general(a, b, (((1,), (1,)), ((), ())), preferred_element_type=F32)


def tn(a, b):
    return lax.dot_general(a, b, (((0,), (0,)), ((), ())), preferred_element_type=F32)


def nn(a, b):
    return jnp.dot(a, b, preferred_element_type=F32)


def call(kernel, outs, args, scratch=(), flops=0, limit=24):
    moved = sum(math.prod(a.shape) * a.dtype.itemsize for a in (*outs, *args))
    return pl.pallas_call(
        kernel,
        out_shape=outs,
        in_specs=[SMEM] + [VMEM] * (len(args) - 1),
        out_specs=[VMEM] * len(outs),
        scratch_shapes=list(scratch),
        compiler_params=pltpu.CompilerParams(vmem_limit_bytes=limit << 20),
        cost_estimate=pl.CostEstimate(flops=flops, bytes_accessed=moved, transcendentals=0),
    )(*args)


def project_kernel(place, blocks, w_own, w_other, kv_out, x, w, total, x_sem, w_sem):
    count, _, depth = blocks.shape
    half = count // 2
    first = place[0] * half

    def block(i):
        return pltpu.make_async_copy(blocks.at[lax.rem(first + i, count)], x.at[i], x_sem.at[i])

    def rows(side, i):
        at = pl.ds(pl.multiple_of(i * depth, depth), depth)
        source = w_own if side == 0 else w_other
        return pltpu.make_async_copy(source.at[at, :], w.at[side, at, :], w_sem.at[side, i])

    for side in range(2):

        @pl.loop(0, half)
        def _(i):
            rows(side, i).start()
            block(side * half + i).start()

    total[...] = jnp.zeros_like(total)
    for side in range(2):

        @pl.loop(0, half)
        def _(i):
            rows(side, i).wait()
            block(side * half + i).wait()
            part = w[side, pl.ds(pl.multiple_of(i * depth, depth), depth), :]
            total[...] += nn(x[side * half + i], part)

    kv_out[...] = total[...].astype(BF16)


def project(place, blocks, weights, weights_other):
    count, rows, depth = blocks.shape
    features, width = weights.shape
    anywhere = pl.BlockSpec(memory_space=pl.ANY)
    return pl.pallas_call(
        project_kernel,
        out_shape=jax.ShapeDtypeStruct((rows, width), BF16),
        in_specs=[SMEM, anywhere, anywhere, anywhere],
        out_specs=VMEM,
        scratch_shapes=[
            pltpu.VMEM((count, rows, depth), BF16),
            pltpu.VMEM((2, features, width), BF16),
            pltpu.VMEM((rows, width), F32),
            pltpu.SemaphoreType.DMA((count,)),
            pltpu.SemaphoreType.DMA((2, count // 2)),
        ],
        compiler_params=pltpu.CompilerParams(vmem_limit_bytes=56 << 20),
        cost_estimate=pl.CostEstimate(
            flops=2 * rows * count * depth * width, bytes_accessed=2 * rows * count * depth, transcendentals=0
        ),
    )(place, blocks, weights, weights_other)


def attention_kernel(place, q_own, do_own, qdo_other, kv_own, kv_other, d_own, d_other, q_all, do_all, kv_all, d_all):
    seq = place[0]
    other = 1 - seq
    rows = q_own.shape[0]
    width = q_own.shape[1]
    for h in range(GROUP):
        at, col = pl.ds(h * rows, rows), pl.ds(h * HEAD_SIZE, HEAD_SIZE)
        q_all[seq, at, :] = q_own[:, col]
        do_all[seq, at, :] = do_own[:, col]
        q_all[other, at, :] = qdo_other[:, col]
        do_all[other, at, :] = qdo_other[:, pl.ds(width + h * HEAD_SIZE, HEAD_SIZE)]
    kv_all[seq] = kv_own[...]
    kv_all[other] = kv_other[...]
    span = 2 * rows
    key_at = lax.broadcasted_iota(jnp.int32, (rows, span), 0)
    query_at = lax.broadcasted_iota(jnp.int32, (rows, span), 1)
    query_at = jnp.where(query_at >= rows, query_at - rows, query_at)
    causal = key_at <= query_at
    d_all[...] = jnp.zeros_like(d_all)
    for block in range(2):

        @pl.loop(0, GROUP * rows // span)
        def _(chunk):
            at = pl.ds(pl.multiple_of(chunk * span, span), span)
            q = q_all[block, at, :]
            do = do_all[block, at, :]
            scores = []
            for j in range(block + 1):
                s = nt(kv_all[j, :, :HEAD_SIZE], q) * SCORE_SCALE
                scores.append(jnp.where(causal, s, F32(-1e30)) if j == block else s)
            peak = functools.reduce(jnp.maximum, [jnp.max(s, axis=0, keepdims=True) for s in scores])
            weights = [jnp.exp(s - peak) for s in scores]
            share = 1.0 / sum(jnp.sum(e, axis=0, keepdims=True) for e in weights)
            probs = [e * share for e in weights]
            low = [p.astype(BF16) for p in probs]
            grads = [nt(kv_all[j, :, HEAD_SIZE:], do) for j in range(block + 1)]
            dot = sum(jnp.sum(p.astype(F32) * g, axis=0, keepdims=True) for p, g in zip(low, grads))
            for j in range(block + 1):
                score_grad = (probs[j] * (grads[j] - dot)).astype(BF16)
                d_all[j, :, :HEAD_SIZE] += nn(score_grad, q)
                d_all[j, :, HEAD_SIZE:] += nn(low[j], do)

    def reduced(at, out):
        out[:, :HEAD_SIZE] = (d_all[at, :, :HEAD_SIZE] * SCORE_SCALE).astype(BF16)
        out[:, HEAD_SIZE:] = d_all[at, :, HEAD_SIZE:].astype(BF16)

    reduced(seq, d_own)
    reduced(other, d_other)


def moment_kernel(part, place, blocks, x_other, d_own, d_other, key_m, value_m, full, low):
    seq = place[0]
    groups, _, depth = x_other.shape
    first = part * groups

    @pl.loop(0, groups)
    def _(i):
        at = pl.ds(pl.multiple_of(i * depth, depth), depth)
        lines = pl.ds(pl.multiple_of((first + i) * depth, depth), depth)
        own = tn(blocks[seq * (blocks.shape[0] // 2) + first + i], d_own[...])
        far = tn(x_other[i], d_other[...])
        grad = own.astype(BF16).astype(F32) + far.astype(BF16).astype(F32)
        m = jnp.concatenate([key_m[lines, :], value_m[lines, :]], axis=1).astype(F32)
        moment = MOMENTUM * m + grad
        full[at, :] = moment
        low[at, :] = moment.astype(BF16)


def average_kernel(parts, place, w_key, w_value, key_far, value_far, *refs):
    full, far, outs = refs[:parts], refs[parts : 2 * parts], refs[2 * parts :]
    lines, head = full[0].shape[0], w_key.shape[1]
    for part in range(parts):

        @pl.loop(0, lines // head)
        def _(i):
            at = pl.ds(pl.multiple_of(i * head, head), head)
            here = pl.ds(pl.multiple_of(part * lines + i * head, head), head)
            moment = 0.5 * (full[part][at, :] + far[part][at, :].astype(F32))
            for k, (w, w_far) in enumerate(((w_key, key_far), (w_value, value_far))):
                new = moment[:, k * head : (k + 1) * head]
                weight = 0.5 * (w[here, :].astype(F32) + w_far[here, :].astype(F32)) - LEARN_RATE * new
                outs[k][0, here, :] = weight.astype(BF16)
                outs[2 + k][0, here, :] = new.astype(BF16)


def after(block, earlier):
    return lax.optimization_barrier((block, earlier))[0]


def swapped(block, axis, distance):
    return lax.ppermute(block, axis, [(i, i ^ distance) for i in range(lax.axis_size(axis))])


def step(bit, tokens, queries, output_gradient, key_matrix, value_matrix, key_velocity, value_velocity):
    tokens, queries, output_gradient = tokens[0], queries[0], output_gradient[0]
    key_w, value_w, key_m, value_m = key_matrix[0], value_matrix[0], key_velocity[0], value_velocity[0]
    rows, depth = tokens.shape
    features, head = key_w.shape
    crowded = bit in CROWDED
    half = lax.axis_size("tp") // 2
    seq = lax.axis_index("seq")
    place = seq.astype(jnp.int32)[None]
    parts = PARTS
    groups, lines = half // parts, features // parts

    blocks = lax.all_gather(tokens, "tp", axis=0, tiled=False)
    weights = jnp.concatenate([key_w, value_w], axis=1)
    qdo = jnp.concatenate([queries, output_gradient], axis=1)
    weights_other = swapped(weights, "seq", 1)
    qdo_other = swapped(qdo, "seq", 1)
    first = weights_other if crowded else weights
    key_far = swapped(after(key_w, first), "rep", 1 << bit)
    value_far = swapped(after(value_w, first), "rep", 1 << bit)

    shape = jax.ShapeDtypeStruct
    if not crowded:
        blocks, qdo_other, key_far, value_far = lax.optimization_barrier((blocks, qdo_other, key_far, value_far))
    kv = project(place, blocks, weights, weights_other)
    kv_other, qdo_other = lax.optimization_barrier((swapped(kv, "seq", 1), qdo_other))
    if crowded:
        kv_other, key_far = lax.optimization_barrier((kv_other, key_far))
    later = after(blocks, kv_other)
    x_other = []
    for part in range(parts):
        sent = lax.dynamic_slice_in_dim(later, (1 - seq) * half + part * groups, groups, axis=0)
        x_other.append(swapped(sent, "seq", 1))
    wide = pltpu.VMEM((2, GROUP * rows, head), BF16)
    d_own, d_other = call(
        attention_kernel,
        [shape((rows, 2 * head), BF16)] * 2,
        [place, queries, output_gradient, qdo_other, kv, kv_other],
        [wide, wide, pltpu.VMEM((2, rows, 2 * head), BF16), pltpu.VMEM((2, rows, 2 * head), F32)],
        flops=2 * 4 * 3 * GROUP * rows * rows * head,
    )
    if crowded:
        d_own, d_other, value_far = lax.optimization_barrier((d_own, d_other, value_far))
    full, far = [], []
    for part in range(parts):
        moment, low = call(
            functools.partial(moment_kernel, part),
            [shape((lines, 2 * head), F32), shape((lines, 2 * head), BF16)],
            [place, blocks, x_other[part], d_own, d_other, key_m, value_m],
            flops=2 * 2 * rows * lines * 2 * head,
        )
        full.append(moment)
        far.append(swapped(low, "rep", 1 << bit))
    return call(
        functools.partial(average_kernel, parts),
        [shape((1, features, head), BF16)] * 4,
        [place, key_w, value_w, key_far, value_far, *full, *far],
    )


def per_device(*args):
    levels = lax.axis_size("rep").bit_length() - 1
    which = jnp.remainder(args[-1][0], jnp.int32(levels))
    return lax.switch(which, [functools.partial(step, bit) for bit in range(levels)], *args[:-1])


def solution(mesh):
    split = P("rep", "seq", "tp")
    return jax.shard_map(
        per_device,
        mesh=mesh,
        in_specs=(split,) * 7 + (P(),),
        out_specs=(split,) * 4,
        check_vma=False,
    )
```

```python
import functools
import math

import jax
import jax.numpy as jnp
from jax import lax
from jax.experimental import pallas as pl
from jax.experimental.pallas import tpu as pltpu
from jax.sharding import PartitionSpec as P

HEAD_SIZE = 128
GROUP = 4
FAR = (2,)
CROWDED = (1, 2)
MOMENTUM = 0.9
LEARN_RATE = 0.01
SCORE_SCALE = 1.0 / math.sqrt(HEAD_SIZE)
F32 = jnp.float32
BF16 = jnp.bfloat16
VMEM = pl.BlockSpec(memory_space=pltpu.VMEM)
SMEM = pl.BlockSpec(memory_space=pltpu.SMEM)


def nt(a, b):
    return lax.dot_general(a, b, (((1,), (1,)), ((), ())), preferred_element_type=F32)


def tn(a, b):
    return lax.dot_general(a, b, (((0,), (0,)), ((), ())), preferred_element_type=F32)


def nn(a, b):
    return jnp.dot(a, b, preferred_element_type=F32)


def call(kernel, outs, args, scratch=(), flops=0, limit=24):
    moved = sum(math.prod(a.shape) * a.dtype.itemsize for a in (*outs, *args))
    return pl.pallas_call(
        kernel,
        out_shape=outs,
        in_specs=[SMEM] + [VMEM] * (len(args) - 1),
        out_specs=[VMEM] * len(outs),
        scratch_shapes=list(scratch),
        compiler_params=pltpu.CompilerParams(vmem_limit_bytes=limit << 20),
        cost_estimate=pl.CostEstimate(flops=flops, bytes_accessed=moved, transcendentals=0),
    )(*args)


def project_kernel(place, blocks, w_own, w_other, kv_out, x, w, total, x_sem, w_sem):
    count, _, depth = blocks.shape
    half = count // 2
    first = place[0] * half

    def block(i):
        return pltpu.make_async_copy(blocks.at[lax.rem(first + i, count)], x.at[i], x_sem.at[i])

    def rows(side, i):
        at = pl.ds(pl.multiple_of(i * depth, depth), depth)
        source = w_own if side == 0 else w_other
        return pltpu.make_async_copy(source.at[at, :], w.at[side, at, :], w_sem.at[side, i])

    for side in range(2):

        @pl.loop(0, half)
        def _(i):
            rows(side, i).start()
            block(side * half + i).start()

    total[...] = jnp.zeros_like(total)
    for side in range(2):

        @pl.loop(0, half)
        def _(i):
            rows(side, i).wait()
            block(side * half + i).wait()
            part = w[side, pl.ds(pl.multiple_of(i * depth, depth), depth), :]
            total[...] += nn(x[side * half + i], part)

    kv_out[...] = total[...].astype(BF16)


def project(place, blocks, weights, weights_other):
    count, rows, depth = blocks.shape
    features, width = weights.shape
    anywhere = pl.BlockSpec(memory_space=pl.ANY)
    return pl.pallas_call(
        project_kernel,
        out_shape=jax.ShapeDtypeStruct((rows, width), BF16),
        in_specs=[SMEM, anywhere, anywhere, anywhere],
        out_specs=VMEM,
        scratch_shapes=[
            pltpu.VMEM((count, rows, depth), BF16),
            pltpu.VMEM((2, features, width), BF16),
            pltpu.VMEM((rows, width), F32),
            pltpu.SemaphoreType.DMA((count,)),
            pltpu.SemaphoreType.DMA((2, count // 2)),
        ],
        compiler_params=pltpu.CompilerParams(vmem_limit_bytes=56 << 20),
        cost_estimate=pl.CostEstimate(
            flops=2 * rows * count * depth * width, bytes_accessed=2 * rows * count * depth, transcendentals=0
        ),
    )(place, blocks, weights, weights_other)


def attention_kernel(place, q_own, do_own, qdo_other, kv_own, kv_other, d_own, d_other, q_all, do_all, kv_all, d_all):
    seq = place[0]
    other = 1 - seq
    rows = q_own.shape[0]
    width = q_own.shape[1]
    for h in range(GROUP):
        at, col = pl.ds(h * rows, rows), pl.ds(h * HEAD_SIZE, HEAD_SIZE)
        q_all[seq, at, :] = q_own[:, col]
        do_all[seq, at, :] = do_own[:, col]
        q_all[other, at, :] = qdo_other[:, col]
        do_all[other, at, :] = qdo_other[:, pl.ds(width + h * HEAD_SIZE, HEAD_SIZE)]
    kv_all[seq] = kv_own[...]
    kv_all[other] = kv_other[...]
    span = 2 * rows
    key_at = lax.broadcasted_iota(jnp.int32, (rows, span), 0)
    query_at = lax.broadcasted_iota(jnp.int32, (rows, span), 1)
    query_at = jnp.where(query_at >= rows, query_at - rows, query_at)
    causal = key_at <= query_at
    d_all[...] = jnp.zeros_like(d_all)
    for block in range(2):

        @pl.loop(0, GROUP * rows // span)
        def _(chunk):
            at = pl.ds(pl.multiple_of(chunk * span, span), span)
            q = q_all[block, at, :]
            do = do_all[block, at, :]
            scores = []
            for j in range(block + 1):
                s = nt(kv_all[j, :, :HEAD_SIZE], q) * SCORE_SCALE
                scores.append(jnp.where(causal, s, F32(-1e30)) if j == block else s)
            peak = functools.reduce(jnp.maximum, [jnp.max(s, axis=0, keepdims=True) for s in scores])
            weights = [jnp.exp(s - peak) for s in scores]
            share = 1.0 / sum(jnp.sum(e, axis=0, keepdims=True) for e in weights)
            probs = [e * share for e in weights]
            low = [p.astype(BF16) for p in probs]
            grads = [nt(kv_all[j, :, HEAD_SIZE:], do) for j in range(block + 1)]
            dot = sum(jnp.sum(p.astype(F32) * g, axis=0, keepdims=True) for p, g in zip(low, grads))
            for j in range(block + 1):
                score_grad = (probs[j] * (grads[j] - dot)).astype(BF16)
                d_all[j, :, :HEAD_SIZE] += nn(score_grad, q)
                d_all[j, :, HEAD_SIZE:] += nn(low[j], do)

    def reduced(at, out):
        out[:, :HEAD_SIZE] = (d_all[at, :, :HEAD_SIZE] * SCORE_SCALE).astype(BF16)
        out[:, HEAD_SIZE:] = d_all[at, :, HEAD_SIZE:].astype(BF16)

    reduced(seq, d_own)
    reduced(other, d_other)


def moment_kernel(group, entry, place, blocks, x_other, d_own, d_other, key_m, value_m, full, low):
    group = place[entry] if group is None else group
    depth = blocks.shape[2]

    @pl.loop(0, 1)
    def _(_):
        own = tn(blocks[place[0] * (blocks.shape[0] // 2) + group], d_own[...])
        far = tn(x_other[0], d_other[...])
        grad = own.astype(BF16).astype(F32) + far.astype(BF16).astype(F32)
        lines = pl.ds(pl.multiple_of(group * depth, depth), depth)
        m = jnp.concatenate([key_m[lines, :], value_m[lines, :]], axis=1).astype(F32)
        moment = MOMENTUM * m + grad
        full[...] = moment
        low[...] = moment.astype(BF16)


def average_kernel(parts, moved, place, w_key, w_value, key_far, value_far, *refs):
    full, far, outs = refs[:parts], refs[parts : 2 * parts], refs[2 * parts :]
    lines, head = full[0].shape[0], w_key.shape[1]
    for part in range(parts):

        @pl.loop(0, lines // head)
        def _(i):
            at = pl.ds(pl.multiple_of(i * head, head), head)
            group = place[1 + part] if moved else part
            here = pl.ds(pl.multiple_of(group * lines + i * head, head), head)
            moment = 0.5 * (full[part][at, :] + far[part][at, :].astype(F32))
            for k, (w, w_far) in enumerate(((w_key, key_far), (w_value, value_far))):
                new = moment[:, k * head : (k + 1) * head]
                weight = 0.5 * (w[here, :].astype(F32) + w_far[here, :].astype(F32)) - LEARN_RATE * new
                outs[k][0, here, :] = weight.astype(BF16)
                outs[2 + k][0, here, :] = new.astype(BF16)


def after(block, earlier):
    return lax.optimization_barrier((block, earlier))[0]


def shifted(block, distance):
    count = lax.axis_size("tp")
    return lax.ppermute(block, "tp", [(i, (i + distance) % count) for i in range(count)])


def swapped(block, axis, distance):
    return lax.ppermute(block, axis, [(i, i ^ distance) for i in range(lax.axis_size(axis))])


def step(bit, tokens, queries, output_gradient, key_matrix, value_matrix, key_velocity, value_velocity):
    tokens, queries, output_gradient = tokens[0], queries[0], output_gradient[0]
    key_w, value_w, key_m, value_m = key_matrix[0], value_matrix[0], key_velocity[0], value_velocity[0]
    rows, depth = tokens.shape
    features, head = key_w.shape
    crowded = bit in CROWDED
    far_apart = bit in FAR
    half = lax.axis_size("tp") // 2
    seq, tp = lax.axis_index("seq"), lax.axis_index("tp")
    order = [jnp.remainder(tp + k + half, half) for k in (0, -1, 1, -2)] if far_apart else list(range(half))
    place = (jnp.stack([seq, *order]) if far_apart else seq[None]).astype(jnp.int32)
    lines = features // half

    blocks = lax.all_gather(tokens, "tp", axis=0, tiled=False)
    weights = jnp.concatenate([key_w, value_w], axis=1)
    qdo = jnp.concatenate([queries, output_gradient], axis=1)
    weights_other = swapped(weights, "seq", 1)
    qdo_other = swapped(qdo, "seq", 1)
    first = weights_other if crowded else weights
    key_far = swapped(after(key_w, first), "rep", 1 << bit)
    if not far_apart:
        value_far = swapped(after(value_w, first), "rep", 1 << bit)

    shape = jax.ShapeDtypeStruct
    if not crowded:
        blocks, qdo_other, key_far, value_far = lax.optimization_barrier((blocks, qdo_other, key_far, value_far))
    kv = project(place, blocks, weights, weights_other)
    kv_other, qdo_other = lax.optimization_barrier((swapped(kv, "seq", 1), qdo_other))
    if crowded:
        kv_other, key_far = lax.optimization_barrier((kv_other, key_far))
    later = after(blocks, kv_other)
    x_other = []
    for group in order[:1] if far_apart else order:
        sent = lax.dynamic_slice_in_dim(later, (1 - seq) * half + group, 1, axis=0)
        x_other.append(swapped(sent, "seq", 1))
    if far_apart:
        value_far = swapped(after(value_w, x_other[0]), "rep", 1 << bit)
    wide = pltpu.VMEM((2, GROUP * rows, head), BF16)
    d_own, d_other = call(
        attention_kernel,
        [shape((rows, 2 * head), BF16)] * 2,
        [place, queries, output_gradient, qdo_other, kv, kv_other],
        [wide, wide, pltpu.VMEM((2, rows, 2 * head), BF16), pltpu.VMEM((2, rows, 2 * head), F32)],
        flops=2 * 4 * 3 * GROUP * rows * rows * head,
    )
    if far_apart:
        near = after(x_other[0], d_own)
        x_other += [shifted(near, 1), shifted(near, -1)]
        x_other.append(shifted(x_other[1], 1))
        x_other[3], value_far = lax.optimization_barrier((x_other[3], value_far))
    elif crowded:
        d_own, d_other, value_far = lax.optimization_barrier((d_own, d_other, value_far))
    full, far = [], []
    for part in range(half):
        moment, low = call(
            functools.partial(moment_kernel, None if far_apart else order[part], 1 + part),
            [shape((lines, 2 * head), F32), shape((lines, 2 * head), BF16)],
            [place, blocks, x_other[part], d_own, d_other, key_m, value_m],
            flops=2 * 2 * rows * lines * 2 * head,
        )
        full.append(moment)
        far.append(swapped(low, "rep", 1 << bit))
    return call(
        functools.partial(average_kernel, half, far_apart),
        [shape((1, features, head), BF16)] * 4,
        [place, key_w, value_w, key_far, value_far, *full, *far],
    )


def per_device(*args):
    levels = lax.axis_size("rep").bit_length() - 1
    which = jnp.remainder(args[-1][0], jnp.int32(levels))
    return lax.switch(which, [functools.partial(step, bit) for bit in range(levels)], *args[:-1])


def solution(mesh):
    split = P("rep", "seq", "tp")
    return jax.shard_map(
        per_device,
        mesh=mesh,
        in_specs=(split,) * 7 + (P(),),
        out_specs=(split,) * 4,
        check_vma=False,
    )
```

```python
import functools
import math

import jax
import jax.numpy as jnp
from jax import lax
from jax.experimental import pallas as pl
from jax.experimental.pallas import tpu as pltpu
from jax.sharding import PartitionSpec as P

HEAD_SIZE = 128
GROUP = 4
FAR = (2,)
CROWDED = (1, 2)
MOMENTUM = 0.9
LEARN_RATE = 0.01
SCORE_SCALE = 1.0 / math.sqrt(HEAD_SIZE)
F32 = jnp.float32
BF16 = jnp.bfloat16
VMEM = pl.BlockSpec(memory_space=pltpu.VMEM)
SMEM = pl.BlockSpec(memory_space=pltpu.SMEM)


def nt(a, b):
    return lax.dot_general(a, b, (((1,), (1,)), ((), ())), preferred_element_type=F32)


def tn(a, b):
    return lax.dot_general(a, b, (((0,), (0,)), ((), ())), preferred_element_type=F32)


def nn(a, b):
    return jnp.dot(a, b, preferred_element_type=F32)


def call(kernel, outs, args, scratch=(), flops=0, limit=24):
    moved = sum(math.prod(a.shape) * a.dtype.itemsize for a in (*outs, *args))
    return pl.pallas_call(
        kernel,
        out_shape=outs,
        in_specs=[SMEM] + [VMEM] * (len(args) - 1),
        out_specs=[VMEM] * len(outs),
        scratch_shapes=list(scratch),
        compiler_params=pltpu.CompilerParams(vmem_limit_bytes=limit << 20),
        cost_estimate=pl.CostEstimate(flops=flops, bytes_accessed=moved, transcendentals=0),
    )(*args)


def project_kernel(place, blocks, w_own, w_other, kv_out, x, w, total, x_sem, w_sem):
    count, _, depth = blocks.shape
    half = count // 2
    first = place[0] * half

    def block(i):
        return pltpu.make_async_copy(blocks.at[lax.rem(first + i, count)], x.at[i], x_sem.at[i])

    def rows(side, i):
        at = pl.ds(pl.multiple_of(i * depth, depth), depth)
        source = w_own if side == 0 else w_other
        return pltpu.make_async_copy(source.at[at, :], w.at[side, at, :], w_sem.at[side, i])

    for side in range(2):

        @pl.loop(0, half)
        def _(i):
            rows(side, i).start()
            block(side * half + i).start()

    total[...] = jnp.zeros_like(total)
    for side in range(2):

        @pl.loop(0, half)
        def _(i):
            rows(side, i).wait()
            block(side * half + i).wait()
            part = w[side, pl.ds(pl.multiple_of(i * depth, depth), depth), :]
            total[...] += nn(x[side * half + i], part)

    kv_out[...] = total[...].astype(BF16)


def project(place, blocks, weights, weights_other):
    count, rows, depth = blocks.shape
    features, width = weights.shape
    anywhere = pl.BlockSpec(memory_space=pl.ANY)
    return pl.pallas_call(
        project_kernel,
        out_shape=jax.ShapeDtypeStruct((rows, width), BF16),
        in_specs=[SMEM, anywhere, anywhere, anywhere],
        out_specs=VMEM,
        scratch_shapes=[
            pltpu.VMEM((count, rows, depth), BF16),
            pltpu.VMEM((2, features, width), BF16),
            pltpu.VMEM((rows, width), F32),
            pltpu.SemaphoreType.DMA((count,)),
            pltpu.SemaphoreType.DMA((2, count // 2)),
        ],
        compiler_params=pltpu.CompilerParams(vmem_limit_bytes=56 << 20),
        cost_estimate=pl.CostEstimate(
            flops=2 * rows * count * depth * width, bytes_accessed=2 * rows * count * depth, transcendentals=0
        ),
    )(place, blocks, weights, weights_other)


def attention_kernel(place, q_own, do_own, qdo_other, kv_own, kv_other, d_own, d_other, q_all, do_all, kv_all, d_all):
    seq = place[0]
    other = 1 - seq
    rows = q_own.shape[0]
    width = q_own.shape[1]
    for h in range(GROUP):
        at, col = pl.ds(h * rows, rows), pl.ds(h * HEAD_SIZE, HEAD_SIZE)
        q_all[seq, at, :] = q_own[:, col]
        do_all[seq, at, :] = do_own[:, col]
        q_all[other, at, :] = qdo_other[:, col]
        do_all[other, at, :] = qdo_other[:, pl.ds(width + h * HEAD_SIZE, HEAD_SIZE)]
    kv_all[seq] = kv_own[...]
    kv_all[other] = kv_other[...]
    span = 2 * rows
    key_at = lax.broadcasted_iota(jnp.int32, (rows, span), 0)
    query_at = lax.broadcasted_iota(jnp.int32, (rows, span), 1)
    query_at = jnp.where(query_at >= rows, query_at - rows, query_at)
    causal = key_at <= query_at
    d_all[...] = jnp.zeros_like(d_all)
    for block in range(2):

        @pl.loop(0, GROUP * rows // span)
        def _(chunk):
            at = pl.ds(pl.multiple_of(chunk * span, span), span)
            q = q_all[block, at, :]
            do = do_all[block, at, :]
            scores = []
            for j in range(block + 1):
                s = nt(kv_all[j, :, :HEAD_SIZE], q) * SCORE_SCALE
                scores.append(jnp.where(causal, s, F32(-1e30)) if j == block else s)
            peak = functools.reduce(jnp.maximum, [jnp.max(s, axis=0, keepdims=True) for s in scores])
            weights = [jnp.exp(s - peak) for s in scores]
            share = 1.0 / sum(jnp.sum(e, axis=0, keepdims=True) for e in weights)
            probs = [e * share for e in weights]
            low = [p.astype(BF16) for p in probs]
            grads = [nt(kv_all[j, :, HEAD_SIZE:], do) for j in range(block + 1)]
            dot = sum(jnp.sum(p.astype(F32) * g, axis=0, keepdims=True) for p, g in zip(low, grads))
            for j in range(block + 1):
                score_grad = (probs[j] * (grads[j] - dot)).astype(BF16)
                d_all[j, :, :HEAD_SIZE] += nn(score_grad, q)
                d_all[j, :, HEAD_SIZE:] += nn(low[j], do)

    def reduced(at, out):
        out[:, :HEAD_SIZE] = (d_all[at, :, :HEAD_SIZE] * SCORE_SCALE).astype(BF16)
        out[:, HEAD_SIZE:] = d_all[at, :, HEAD_SIZE:].astype(BF16)

    reduced(seq, d_own)
    reduced(other, d_other)


def moment_kernel(group, entry, place, blocks, x_other, d_own, d_other, key_m, value_m, full, low):
    group = place[entry] if group is None else group
    depth = blocks.shape[2]

    @pl.loop(0, 1)
    def _(_):
        own = tn(blocks[place[0] * (blocks.shape[0] // 2) + group], d_own[...])
        far = tn(x_other[0], d_other[...])
        grad = own.astype(BF16).astype(F32) + far.astype(BF16).astype(F32)
        lines = pl.ds(pl.multiple_of(group * depth, depth), depth)
        m = jnp.concatenate([key_m[lines, :], value_m[lines, :]], axis=1).astype(F32)
        moment = MOMENTUM * m + grad
        full[...] = moment
        low[...] = moment.astype(BF16)


def average_kernel(parts, moved, place, w_key, w_value, key_far, value_far, *refs):
    full, far, outs = refs[:parts], refs[parts : 2 * parts], refs[2 * parts :]
    lines, head = full[0].shape[0], w_key.shape[1]
    for part in range(parts):

        @pl.loop(0, lines // head)
        def _(i):
            at = pl.ds(pl.multiple_of(i * head, head), head)
            group = place[1 + part] if moved else part
            here = pl.ds(pl.multiple_of(group * lines + i * head, head), head)
            moment = 0.5 * (full[part][at, :] + far[part][at, :].astype(F32))
            for k, (w, w_far) in enumerate(((w_key, key_far), (w_value, value_far))):
                new = moment[:, k * head : (k + 1) * head]
                weight = 0.5 * (w[here, :].astype(F32) + w_far[here, :].astype(F32)) - LEARN_RATE * new
                outs[k][0, here, :] = weight.astype(BF16)
                outs[2 + k][0, here, :] = new.astype(BF16)


def after(block, earlier):
    return lax.optimization_barrier((block, earlier))[0]


def shifted(block, distance):
    count = lax.axis_size("tp")
    return lax.ppermute(block, "tp", [(i, (i + distance) % count) for i in range(count)])


def swapped(block, axis, distance):
    return lax.ppermute(block, axis, [(i, i ^ distance) for i in range(lax.axis_size(axis))])


def step(bit, tokens, queries, output_gradient, key_matrix, value_matrix, key_velocity, value_velocity):
    tokens, queries, output_gradient = tokens[0], queries[0], output_gradient[0]
    key_w, value_w, key_m, value_m = key_matrix[0], value_matrix[0], key_velocity[0], value_velocity[0]
    rows, depth = tokens.shape
    features, head = key_w.shape
    crowded = bit in CROWDED
    far_apart = bit in FAR
    half = lax.axis_size("tp") // 2
    seq, tp = lax.axis_index("seq"), lax.axis_index("tp")
    order = [jnp.remainder(tp + k + half, half) for k in (0, -1, 1, -2)] if far_apart else list(range(half))
    place = (jnp.stack([seq, *order]) if far_apart else seq[None]).astype(jnp.int32)
    lines = features // half

    blocks = lax.all_gather(tokens, "tp", axis=0, tiled=False)
    weights = jnp.concatenate([key_w, value_w], axis=1)
    qdo = jnp.concatenate([queries, output_gradient], axis=1)
    weights_other = swapped(weights, "seq", 1)
    qdo_other = swapped(qdo, "seq", 1)
    first = weights_other if crowded else weights
    key_far = swapped(after(key_w, first), "rep", 1 << bit)
    if not far_apart:
        value_far = swapped(after(value_w, first), "rep", 1 << bit)

    shape = jax.ShapeDtypeStruct
    if not crowded:
        blocks, qdo_other, key_far, value_far = lax.optimization_barrier((blocks, qdo_other, key_far, value_far))
    kv = project(place, blocks, weights, weights_other)
    kv_other, qdo_other = lax.optimization_barrier((swapped(kv, "seq", 1), qdo_other))
    if crowded:
        kv_other, key_far = lax.optimization_barrier((kv_other, key_far))
    later = after(blocks, kv_other)
    soon = later if crowded else after(blocks, kv)
    x_other = []
    for group in order[:1] if far_apart else order:
        held = later if x_other else soon
        sent = lax.dynamic_slice_in_dim(held, (1 - seq) * half + group, 1, axis=0)
        x_other.append(swapped(sent, "seq", 1))
    if far_apart:
        value_far = swapped(after(value_w, x_other[0]), "rep", 1 << bit)
    wide = pltpu.VMEM((2, GROUP * rows, head), BF16)
    d_own, d_other = call(
        attention_kernel,
        [shape((rows, 2 * head), BF16)] * 2,
        [place, queries, output_gradient, qdo_other, kv, kv_other],
        [wide, wide, pltpu.VMEM((2, rows, 2 * head), BF16), pltpu.VMEM((2, rows, 2 * head), F32)],
        flops=2 * 4 * 3 * GROUP * rows * rows * head,
    )
    if far_apart:
        near = after(x_other[0], d_own)
        x_other += [shifted(near, 1), shifted(near, -1)]
        x_other.append(shifted(x_other[1], 1))
        x_other[3], value_far = lax.optimization_barrier((x_other[3], value_far))
    elif crowded:
        d_own, d_other, value_far = lax.optimization_barrier((d_own, d_other, value_far))
    full, far = [], []
    for part in range(half):
        moment, low = call(
            functools.partial(moment_kernel, None if far_apart else order[part], 1 + part),
            [shape((lines, 2 * head), F32), shape((lines, 2 * head), BF16)],
            [place, blocks, x_other[part], d_own, d_other, key_m, value_m],
            flops=2 * 2 * rows * lines * 2 * head,
        )
        full.append(moment)
        far.append(swapped(low, "rep", 1 << bit))
    return call(
        functools.partial(average_kernel, half, far_apart),
        [shape((1, features, head), BF16)] * 4,
        [place, key_w, value_w, key_far, value_far, *full, *far],
    )


def per_device(*args):
    levels = lax.axis_size("rep").bit_length() - 1
    which = jnp.remainder(args[-1][0], jnp.int32(levels))
    return lax.switch(which, [functools.partial(step, bit) for bit in range(levels)], *args[:-1])


def solution(mesh):
    split = P("rep", "seq", "tp")
    return jax.shard_map(
        per_device,
        mesh=mesh,
        in_specs=(split,) * 7 + (P(),),
        out_specs=(split,) * 4,
        check_vma=False,
    )
```
